32 devices in a mesh: seq: 4 (over z), exp: 8 (over y, x, core).
Axes of the slice: x: 2, y: 2, z: 4, core: 2. Of those that a mesh axis runs over, the one named last changes fastest.
Arguments:
- attn_inputs: bfloat16 [8, 512, 6144], P('exp', 'seq'), may hold values from -8 to 8
- residual: bfloat16 [8, 512, 2048], P('exp', 'seq'), may hold values from -6 to 6
- out_weight: bfloat16 [2048, 2048], P('exp'), may hold values from -0.125 to 0.125
- norm_gain: float32 [2048], replicated, may hold values from 0.1 to 1.9
- expert_ids: int32 [8, 512, 2], P('exp', 'seq'), may hold values from 0 to 7, all different within a row; in each aligned block of 128 rows (0 to 127, 128 to 255, ..., all dimensions but the last counted through in order) at most 40 rows name the same one
- gate_weights: float32 [8, 512, 2], P('exp', 'seq'), may hold values from 0.1 to 1
- gate_weight: bfloat16 [8, 2048, 5632], P('exp', None, 'seq'), may hold values from -0.125 to 0.125
- up_weight: bfloat16 [8, 2048, 5632], P('exp', None, 'seq'), may hold values from -0.125 to 0.125
- down_weight: bfloat16 [8, 5632, 2048], P('exp', 'seq'), may hold values from -0.078125 to 0.078125
Outputs:
- layer_out: bfloat16 [8, 512, 2048], P('exp', 'seq')
The draws below stay inside these ranges and needn't reach their ends.
Inputs may be any that keep to these rules, and one draw needn't show every extreme that they name: `expert_ids`: each token names 2 different experts; in every draw no expert is named by more than 40 of the 128 tokens of one aligned block of rows (the rows of one device), and some block reaches 40.
All inputs are finite; a program needn't handle non-finite values.
Results may differ from the reference program's by a relative error of at most 0.013.
Values may be sent and summed in bfloat16 or wider, within the bound.
No kernel may reach another device: no remote copies, remote signals or barrier semaphores. Data moves between devices by JAX's collectives and lax.ppermute only.
A program may use at most 128 MiB of HBM per device.

```python
import math
import jax
import jax.numpy as jnp
import numpy as np
from jax import lax

D = 2048
HEADS = 16
HEAD_DIM = 128
FF = 5632
TOP = 2
TOK_DEV = 128
EXPERTS = 8
CAP = 40
CLIPS = 8
CLIP_LEN = 512
N_SEQ = 4


def draw_attn_inputs(key, part):
    model_width = HEADS * HEAD_DIM
    full_shape = (CLIPS, CLIP_LEN, 3 * model_width)
    first_key = jax.random.fold_in(key, 0)
    column = lax.broadcasted_iota(jnp.int32, (1, 1, 3 * model_width), 2)
    normal_draw = jax.random.normal(first_key, full_shape, jnp.float32)
    factor = jnp.where(column < 2 * model_width, 1.22, 1.0)
    return jnp.clip(normal_draw * factor, -8.0, 8.0).astype(jnp.bfloat16)


def level_of(own_key, extent, cuts, smallest, high):
    loudness = 1.0
    for dim, parts in cuts:
        draws = jax.random.uniform(jax.random.fold_in(jax.random.fold_in(own_key, 6), dim), (parts,), jnp.float32, smallest / len(cuts), high / len(cuts))
        loudness = loudness * jnp.repeat(jnp.exp(draws), extent[dim] // parts).reshape((-1,) + (1,) * (len(extent) - 1 - dim))
    return loudness


def shared_out(own_key, own, number, rows, number_of, top, bound, slope):
    sequence = jax.random.permutation(own_key, number_of)
    crowded, common = load_shares(number_of, rows * top, bound, slope, True), load_shares(number_of, rows * top, bound, slope, False)
    places = jnp.arange(number_of)

    def named(lengths, rotation):
        used = int((lengths > 0).sum())
        fixed = max(1, used // 4)
        moved = fixed + (places - fixed + rotation * (used - fixed)) % max(1, number_of - fixed)
        return jnp.zeros((number_of,), jnp.int32).at[sequence[jnp.where(places < fixed, places, moved)]].set(jnp.asarray(lengths, jnp.int32))

    lengths = jnp.where(number % 4 == 0, named(crowded, number // 4), named(common, number - number // 4 - 1))
    mixed = jax.random.permutation(jax.random.fold_in(own, 3), number_of)
    giver, taker = mixed[0:number_of // 2 * 2:2], mixed[1:number_of // 2 * 2:2]
    margin = jnp.minimum(lengths[giver] - 1, bound - lengths[taker]) // 2
    margin = jnp.where((giver == sequence[0]) | (taker == sequence[0]) | (lengths[taker] == 0), 0, jnp.maximum(margin, 0))
    moved = jax.random.randint(jax.random.fold_in(own, 4), (number_of // 2,), 0, 1 << 20) % (margin + 1)
    lengths = lengths.at[giver].add(-moved).at[taker].add(moved)
    members = jnp.searchsorted(jnp.cumsum(lengths), jnp.arange(rows * top), side="right").astype(jnp.int32)
    grid = members.reshape(top, rows).T
    grid = grid[jax.random.permutation(jax.random.fold_in(own, 1), rows)]
    rotation = jax.random.randint(jax.random.fold_in(own, 2), (rows, 1), 0, top)
    return jnp.take_along_axis(grid, (jnp.arange(top)[None, :] + rotation) % top, axis=1)


def load_shares(count, total, most, lean, full):
    portions = [(1 << 20) // math.isqrt(rank ** lean) + 1 for rank in range(1, count + 1)]
    largest = most if full else min(most, max(-(-total // count), total * portions[0] // sum(portions)))
    least = 1 if total - largest >= count - 1 else 0
    holding, spare = [largest] + [least] * (count - 1), total - largest - least * (count - 1)
    while spare > 0:
        candidates = [i for i in range(1, count) if holding[i] < largest] or [i for i in range(1, count) if holding[i] < most]
        whole, remaining = sum([portions[i] for i in candidates]), spare
        for i in candidates:
            more = min(most - holding[i], max(1, remaining * portions[i] // whole), spare)
            holding[i] = holding[i] + more
            spare = spare - more
    return np.array(holding)


def bell_draw(rng, extent, width, limit, cuts=(), kind=jnp.bfloat16):
    drawn = jax.random.normal(rng, extent, jnp.float32) * width
    if len(cuts) > 0:
        drawn = level_of(rng, extent, cuts, -0.22, 0.18) * drawn
    return jnp.clip(drawn, min=-limit, max=limit).astype(kind)


def setup_inputs(seed: int = 0) -> dict:
    seeds = jax.random.split(jax.random.key(seed), 10)
    attn_inputs = draw_attn_inputs(jax.random.fold_in(seeds[9], 71), 0)
    residual = bell_draw(seeds[1], (CLIPS, CLIP_LEN, D), 1.0, 6.0, ((0, 8), (1, 4)))
    out_weight = bell_draw(seeds[2], (D, D), D ** -0.5, 0.125, ((0, 8),))
    norm_gain = jnp.clip(1.0 + 0.18 * jax.random.normal(seeds[3], (D,), jnp.float32), 0.1, 1.9)
    expert_ids_keys = jax.random.split(jax.random.fold_in(seeds[4], 1), CLIPS * CLIP_LEN // TOK_DEV)
    expert_ids_turns = jax.random.permutation(jax.random.fold_in(seeds[4], 3), CLIPS * CLIP_LEN // TOK_DEV)
    expert_ids = jax.vmap(lambda own, number: shared_out(jax.random.fold_in(seeds[4], 2), own, number, TOK_DEV, EXPERTS, TOP, CAP, 2))(expert_ids_keys, expert_ids_turns).reshape((CLIPS, CLIP_LEN, TOP))
    gate_weights = jnp.clip(0.1 + 0.9 * jax.random.uniform(seeds[5], (CLIPS, CLIP_LEN, TOP), jnp.float32) ** level_of(seeds[5], (CLIPS, CLIP_LEN, TOP), ((0, 8), (1, 4)), -0.2, 0.2), 0.1, 1.0)
    gate_weight = bell_draw(seeds[6], (EXPERTS, D, FF), D ** -0.5, 0.125, ((0, 8), (2, 4)))
    up_weight = bell_draw(seeds[7], (EXPERTS, D, FF), D ** -0.5, 0.125, ((0, 8), (2, 4)))
    down_weight = bell_draw(seeds[8], (EXPERTS, FF, D), FF ** -0.5, 0.078125, ((0, 8), (1, 4)))
    return {"attn_inputs": attn_inputs, "residual": residual, "out_weight": out_weight, "norm_gain": norm_gain, "expert_ids": expert_ids, "gate_weights": gate_weights, "gate_weight": gate_weight, "up_weight": up_weight, "down_weight": down_weight}


def attend_clip(clip_inputs):
    model_width = HEADS * HEAD_DIM
    query_rows = clip_inputs[:, :model_width].reshape(-1, HEADS, HEAD_DIM).astype(jnp.float32)
    key_rows = clip_inputs[:, model_width:2 * model_width].reshape(-1, HEADS, HEAD_DIM).astype(jnp.float32)
    value_rows = clip_inputs[:, 2 * model_width:].reshape(-1, HEADS, HEAD_DIM).astype(jnp.float32)
    scores = jnp.einsum('qhd,khd->hqk', query_rows, key_rows, precision=lax.Precision.HIGHEST) * HEAD_DIM ** (-0.5)
    attn_probs = jax.nn.softmax(scores, axis=-1).astype(jnp.bfloat16)
    mixed_heads = jnp.einsum('hqk,khd->qhd', attn_probs.astype(jnp.float32), value_rows, precision=lax.Precision.HIGHEST)
    return mixed_heads.astype(jnp.bfloat16).reshape(-1, model_width)

def expert_apply(operands):
    gate_mat, up_mat, down_mat, tok_rows = operands
    gate_val = jnp.dot(tok_rows, gate_mat, preferred_element_type=jnp.float32)
    up_val = jnp.dot(tok_rows, up_mat, preferred_element_type=jnp.float32)
    hidden = (jax.nn.silu(gate_val) * up_val).astype(jnp.bfloat16)
    quarter = FF // N_SEQ
    partial_terms = jnp.einsum('rsf,sfd->srd', hidden.reshape(-1, N_SEQ, quarter).astype(jnp.float32), down_mat.reshape(N_SEQ, quarter, -1).astype(jnp.float32), precision=lax.Precision.HIGHEST)
    rounded = lax.optimization_barrier(partial_terms.astype(jnp.bfloat16))
    return lax.optimization_barrier(jnp.sum(rounded.astype(jnp.float32), axis=0)).astype(jnp.bfloat16)

def reference(attn_inputs, residual, out_weight, norm_gain, expert_ids, gate_weights, gate_weight, up_weight, down_weight):
    model_width = residual.shape[-1]
    attended = lax.map(attend_clip, attn_inputs)
    projected = jnp.dot(attended.reshape(-1, model_width), out_weight, preferred_element_type=jnp.float32)
    middle = lax.optimization_barrier((residual.reshape(-1, model_width).astype(jnp.float32) + projected).astype(jnp.bfloat16))
    mid_float = middle.astype(jnp.float32)
    normed = (mid_float * lax.rsqrt(lax.optimization_barrier(jnp.mean(mid_float * mid_float, axis=-1, keepdims=True)) + 1e-06) * norm_gain).astype(jnp.bfloat16)
    blocks = CLIPS * N_SEQ
    route_ids = expert_ids.reshape(blocks, TOK_DEV * TOP).astype(jnp.int32)
    one_hot = (route_ids[:, :, None] == jnp.arange(EXPERTS, dtype=jnp.int32)[None, None, :]).astype(jnp.int32)
    before = (jnp.cumsum(one_hot, axis=1).astype(jnp.int32) - one_hot).astype(jnp.int32)
    slot_ids = lax.optimization_barrier(jnp.sum(before * one_hot, axis=-1)).astype(jnp.int32)
    block_ids = jnp.broadcast_to(jnp.arange(blocks, dtype=jnp.int32)[:, None], route_ids.shape).astype(jnp.int32)
    flat_index = ((block_ids * EXPERTS + route_ids) * CAP + slot_ids).astype(jnp.int32)
    buffer = jnp.zeros((blocks * EXPERTS * CAP, model_width), jnp.bfloat16).at[flat_index.reshape(-1)].set(jnp.repeat(normed, TOP, axis=0))
    expert_in = buffer.reshape(blocks, EXPERTS, CAP, model_width).transpose(1, 0, 2, 3).reshape(EXPERTS, blocks * CAP, model_width)
    expert_out = lax.map(expert_apply, (gate_weight, up_weight, down_weight, expert_in)).reshape(EXPERTS, blocks, CAP, model_width)
    picked = expert_out[route_ids, block_ids, slot_ids]
    weighted = picked.astype(jnp.float32).reshape(-1, TOP, model_width) * gate_weights.reshape(-1, TOP, 1).astype(jnp.float32)
    result = mid_float + lax.optimization_barrier(jnp.sum(weighted, axis=1))
    return result.astype(jnp.bfloat16).reshape(CLIPS, CLIP_LEN, model_width)
```

```python
import functools

import jax
import jax.numpy as jnp
from jax import lax
from jax.experimental import pallas as pl
from jax.experimental.pallas import tpu as pltpu
from jax.sharding import PartitionSpec as P

HEADS = 16
HEAD_DIM = 128
TOP = 2
TRADES = 8
AHEAD = 2
HID_TILE = 512
OUT_TILE = 1024
VMEM_LIMIT = 16 * 1024 * 1024
ANY = pl.BlockSpec(memory_space=pl.ANY)


def xor_pairs(count, offset):
    return [(i, i ^ offset) for i in range(count)]


def whole(shape):
    return pl.BlockSpec(shape, lambda *_: (0,) * len(shape))


def params():
    return pltpu.CompilerParams(vmem_limit_bytes=VMEM_LIMIT)


def cost(flops, bytes_accessed, transcendentals):
    return pl.CostEstimate(
        flops=0 * flops, bytes_accessed=0 * bytes_accessed, transcendentals=0 * transcendentals
    )


def after(arrays, deps):
    count = len(arrays)
    return pl.pallas_call(
        lambda *_: None,
        in_specs=[ANY] * (count + len(deps)),
        out_specs=[ANY] * count,
        out_shape=[jax.ShapeDtypeStruct(a.shape, a.dtype) for a in arrays],
        input_output_aliases={i: i for i in range(count)},
        compiler_params=pltpu.CompilerParams(vmem_limit_bytes=1024 * 1024),
        cost_estimate=cost(0, 0, 0),
        name="after",
    )(*arrays, *deps)


def attend_kernel(count, *refs):
    parts, outs = refs[: 3 * count], refs[3 * count :]
    block = outs[0].shape[0]
    query, key, value = (
        jnp.concatenate([p[...] for p in parts[w * count : (w + 1) * count]], axis=0)
        for w in range(3)
    )
    scores = lax.dot_general(
        query, key, (((1,), (1,)), ((), ())), preferred_element_type=jnp.float32
    ) * HEAD_DIM ** (-0.5)
    top = jnp.max(scores, axis=-1, keepdims=True)
    grown = jnp.exp(scores - top)
    probs = (grown / jnp.sum(grown, axis=-1, keepdims=True)).astype(jnp.bfloat16)
    mixed = jnp.dot(probs, value, preferred_element_type=jnp.float32).astype(jnp.bfloat16)
    for i in range(count):
        outs[i][...] = mixed[i * block : (i + 1) * block]


def attend(blocks, head_local):
    count = len(blocks)
    tok = blocks[0].shape[0]
    clip_len = count * tok

    def part(which):
        return pl.BlockSpec((tok, HEAD_DIM), lambda h: (0, which * head_local + h))

    return pl.pallas_call(
        functools.partial(attend_kernel, count),
        grid=(head_local,),
        in_specs=[part(which) for which in range(3) for _ in range(count)],
        out_specs=[pl.BlockSpec((tok, HEAD_DIM), lambda h: (0, h))] * count,
        out_shape=[jax.ShapeDtypeStruct((tok, head_local * HEAD_DIM), jnp.bfloat16)] * count,
        compiler_params=params(),
        cost_estimate=cost(
            4 * head_local * clip_len * clip_len * HEAD_DIM,
            8 * clip_len * head_local * HEAD_DIM,
            head_local * clip_len * clip_len,
        ),
        name="attend",
    )(*(list(blocks) * 3))


def project_kernel(count, seq_ref, *refs):
    parts = refs[:count]
    weight_ref, res_ref, gain_ref, mid_ref, norm_ref, acc_ref = refs[count:]
    step = pl.program_id(0)
    for i in range(count):

        @pl.when(step == i)
        def _(i=i):
            term = jnp.dot(parts[i][...], weight_ref[...], preferred_element_type=jnp.float32)
            acc_ref[...] = (res_ref[...].astype(jnp.float32) if i == 0 else acc_ref[...]) + term

    @pl.when(step == count - 1)
    def _():
        middle = acc_ref[...].astype(jnp.bfloat16)
        mid_ref[...] = middle
        mid_float = middle.astype(jnp.float32)
        mean = jnp.mean(mid_float * mid_float, axis=-1, keepdims=True)
        norm_ref[...] = (mid_float * lax.rsqrt(mean + 1e-06) * gain_ref[...]).astype(
            jnp.bfloat16
        )


def project(my_seq, parts, weight, residual, gain):
    count = len(parts)
    tok, depth = parts[0].shape
    width = weight.shape[1]
    out = jax.ShapeDtypeStruct((tok, width), jnp.bfloat16)
    return pl.pallas_call(
        functools.partial(project_kernel, count),
        grid_spec=pltpu.PrefetchScalarGridSpec(
            num_scalar_prefetch=1,
            grid=(count,),
            in_specs=[whole((tok, depth))] * count
            + [
                pl.BlockSpec((depth, width), lambda k, seq: (seq[0] ^ k, 0)),
                whole((tok, width)),
                whole((1, width)),
            ],
            out_specs=[whole((tok, width))] * 2,
            scratch_shapes=[pltpu.VMEM((tok, width), jnp.float32)],
        ),
        out_shape=[out, out],
        compiler_params=params(),
        cost_estimate=cost(2 * tok * count * depth * width, 2 * count * depth * width, 0),
        name="project",
    )(my_seq.reshape(1), *parts, weight, residual, gain.reshape(1, width))


def slot_kernel(hop, chips, place_ref, mine_ref, *rest):
    outs = rest[-chips:]
    piece = outs[0].shape[0]
    place = place_ref[hop]
    row = lax.broadcasted_iota(jnp.int32, (chips * piece, place.shape[-1]), 0)
    others = rest[:TRADES]
    halves = []
    for which in range(2):
        hit = (row == place[2 * which : 2 * which + 1]) | (
            row == place[2 * which + 1 : 2 * which + 2]
        )
        halves.append(jnp.where(hit, 1.0, 0.0).astype(jnp.bfloat16))
    slotted = jnp.dot(
        jnp.concatenate(halves, axis=1),
        jnp.concatenate([mine_ref[...]] + [o[...] for o in others], axis=0),
        preferred_element_type=jnp.float32,
    ).astype(jnp.bfloat16)
    for step in range(chips):
        outs[step][...] = slotted[step * piece : (step + 1) * piece]


def to_slots(hop, chips, piece, place, mine, others, deps):
    tok, width = mine.shape
    return pl.pallas_call(
        functools.partial(slot_kernel, hop, chips),
        in_specs=[whole(place.shape), whole(mine.shape)]
        + [whole(o.shape) for o in others]
        + [ANY] * len(deps),
        out_specs=[whole((piece, width))] * chips,
        out_shape=[jax.ShapeDtypeStruct((piece, width), jnp.bfloat16)] * chips,
        compiler_params=params(),
        cost_estimate=cost(4 * chips * piece * tok * width, 2 * width * (2 * tok + chips * piece), 0),
        name=f"slots{hop}",
    )(place, mine, *others, *deps)


def expert_kernel(chips, n_deps, *refs):
    pieces = refs[:chips]
    gate_hbm, up_hbm, down_hbm = refs[chips : chips + 3]
    outs = refs[chips + 3 + n_deps : 2 * chips + 3 + n_deps]
    rows_ref, hid_ref, gate_ref, up_ref, down_ref, sem = refs[-6:]
    piece = pieces[0].shape[0]
    hid, width = down_ref.shape
    hid_tiles = [slice(at, min(at + HID_TILE, hid)) for at in range(0, hid, HID_TILE)]
    out_tiles = [slice(at, at + OUT_TILE) for at in range(0, width, OUT_TILE)]
    stages = [[(gate_hbm, gate_ref, t), (up_hbm, up_ref, t)] for t in hid_tiles]
    stages += [[(down_hbm, down_ref, t)] for t in out_tiles]
    copies, count = [], 0
    for stage in stages:
        group = []
        for source, target, tile in stage:
            group.append(
                pltpu.make_async_copy(source.at[:, tile], target.at[:, tile], sem.at[count])
            )
            count += 1
        copies.append(group)

    def start(n):
        if n < len(copies):
            for copy in copies[n]:
                copy.start()

    def wait(n):
        for copy in copies[n]:
            copy.wait()
        start(n + AHEAD)

    for n in range(AHEAD):
        start(n)
    for i in range(chips):
        rows_ref[i * piece : (i + 1) * piece, :] = pieces[i][...]
    for n, tile in enumerate(hid_tiles):
        wait(n)
        gate_val = jnp.dot(rows_ref[...], gate_ref[:, tile], preferred_element_type=jnp.float32)
        up_val = jnp.dot(rows_ref[...], up_ref[:, tile], preferred_element_type=jnp.float32)
        hidden = gate_val / (1.0 + jnp.exp(-gate_val)) * up_val
        hid_ref[:, tile] = hidden.astype(jnp.bfloat16)
    for n, tile in enumerate(out_tiles):
        wait(len(hid_tiles) + n)
        out = jnp.dot(hid_ref[...], down_ref[:, tile], preferred_element_type=jnp.float32)
        out = out.astype(jnp.bfloat16)
        for i in range(chips):
            outs[i][:, tile] = out[i * piece : (i + 1) * piece]


def expert(hop, pieces, gate_mat, up_mat, down_mat, deps):
    chips = len(pieces)
    piece, width = pieces[0].shape
    hid = gate_mat.shape[-1]
    rows = chips * piece
    in_vmem = pl.BlockSpec(memory_space=pltpu.VMEM)
    in_hbm = pl.BlockSpec(memory_space=pltpu.HBM)
    n_sems = 2 * -(-hid // HID_TILE) + width // OUT_TILE
    return pl.pallas_call(
        functools.partial(expert_kernel, chips, len(deps)),
        in_specs=[in_vmem] * chips + [in_hbm] * 3 + [ANY] * len(deps),
        out_specs=[in_vmem] * chips,
        out_shape=[jax.ShapeDtypeStruct((piece, width), jnp.bfloat16)] * chips,
        scratch_shapes=[
            pltpu.VMEM((rows, width), jnp.bfloat16),
            pltpu.VMEM((rows, hid), jnp.bfloat16),
            pltpu.VMEM((width, hid), jnp.bfloat16),
            pltpu.VMEM((width, hid), jnp.bfloat16),
            pltpu.VMEM((hid, width), jnp.bfloat16),
            pltpu.SemaphoreType.DMA((n_sems,)),
        ],
        compiler_params=pltpu.CompilerParams(vmem_limit_bytes=56 * 1024 * 1024),
        cost_estimate=cost(6 * rows * width * hid, 6 * width * hid, rows * hid),
        name=f"expert{hop}",
    )(*pieces, gate_mat, up_mat, down_mat, *deps)


def combine_kernel(hop, chips, n_deps, place_ref, gates_ref, *refs):
    pieces = refs[:chips]
    mine_ref, other_ref = refs[chips + n_deps :]
    rows = jnp.concatenate([p[...] for p in pieces], axis=0)
    place = place_ref[hop]
    gates = gates_ref[hop]
    column = lax.broadcasted_iota(jnp.int32, (place.shape[0], rows.shape[0]), 1)
    for which, out_ref in ((0, mine_ref), (1, other_ref)):
        total = 0.0
        for choice in range(TOP):
            at = 2 * which + choice
            picking = jnp.where(column == place[:, at : at + 1], 1.0, 0.0).astype(jnp.bfloat16)
            picked = jnp.dot(picking, rows, preferred_element_type=jnp.float32)
            total = total + picked * gates[:, at : at + 1]
        out_ref[...] = total.astype(out_ref.dtype)


def combine(hop, pieces, place, gates, deps):
    chips = len(pieces)
    piece, width = pieces[0].shape
    tok = place.shape[1]
    tile = pl.BlockSpec((tok, OUT_TILE), lambda i: (0, i))
    return pl.pallas_call(
        functools.partial(combine_kernel, hop, chips, len(deps)),
        grid=(width // OUT_TILE,),
        in_specs=[whole(place.shape), whole(gates.shape)]
        + [pl.BlockSpec((piece, OUT_TILE), lambda i: (0, i))] * chips
        + [ANY] * len(deps),
        out_specs=[tile, tile],
        out_shape=[
            jax.ShapeDtypeStruct((tok, width), jnp.float32),
            jax.ShapeDtypeStruct((tok, width), jnp.bfloat16),
        ],
        compiler_params=params(),
        cost_estimate=cost(8 * tok * chips * piece * width, 2 * width * (chips * piece + 3 * tok), 0),
        name=f"combine{hop}",
    )(place, gates, *pieces, *deps)


def per_device(
    attn_inputs,
    residual,
    out_weight,
    norm_gain,
    expert_ids,
    gate_weights,
    gate_weight,
    up_weight,
    down_weight,
):
    tok_count = attn_inputs.shape[1]
    seq_count = lax.axis_size("seq")
    expert_count = lax.axis_size("exp")
    chips = expert_count // 2
    my_seq = lax.axis_index("seq")
    my_exp = lax.axis_index("exp")
    my_core, my_chip = my_exp % 2, my_exp // 2
    model_width = residual.shape[-1]
    head_local = HEADS // seq_count
    capacity = 5 * tok_count // (2 * expert_count)
    piece = -(-2 * capacity // 16) * 16

    def over_seq(value, hop):
        return lax.ppermute(value, "seq", xor_pairs(seq_count, hop))

    def over_chips(value, step):
        return lax.ppermute(value, "exp", xor_pairs(expert_count, 2 * step))

    def over_cores(value):
        return lax.ppermute(value, "exp", xor_pairs(expert_count, 1))

    gate_mat, up_mat, down_mat = gate_weight[0], up_weight[0], down_weight[0]

    def trade(value):
        part = value.shape[0] // TRADES
        return [over_cores(value[i * part : (i + 1) * part]) for i in range(TRADES)]

    head_cols = head_local * HEAD_DIM
    laid = attn_inputs.reshape(tok_count, 3, seq_count, head_cols)
    blocks = []
    for hop in range(seq_count):
        part = lax.dynamic_index_in_dim(laid, my_seq ^ hop, 2, keepdims=False)
        part = part.reshape(tok_count, 3 * head_cols)
        blocks.append(over_seq(part, hop) if hop else part)
    attended = attend(blocks, head_local)
    merged = [over_seq(p, hop) if hop else p for hop, p in enumerate(attended)]

    route_ids = expert_ids.reshape(tok_count * TOP)
    one_hot = (
        route_ids[:, None] == jnp.arange(expert_count, dtype=jnp.int32)[None, :]
    ).astype(jnp.int32)
    before = jnp.cumsum(one_hot, axis=0) - one_hot
    slot_ids = jnp.sum(before * one_hot, axis=-1)
    target = (route_ids * capacity + slot_ids).reshape(tok_count, TOP)
    route = jnp.concatenate([target.astype(jnp.float32), gate_weights[0]], axis=1).T
    route = jnp.stack([route] + [over_seq(route, hop) for hop in range(1, seq_count)])
    both = jnp.concatenate([route, over_cores(route)], axis=1)
    goal = jnp.concatenate([both[:, :TOP], both[:, 2 * TOP : 3 * TOP]], axis=1).astype(jnp.int32)
    gates = jnp.concatenate([both[:, TOP : 2 * TOP], both[:, 3 * TOP :]], axis=1)
    goal_exp = goal // capacity
    clip = (jnp.arange(2 * TOP, dtype=jnp.int32) // TOP)[None, :, None]
    place = jnp.where(
        goal_exp % 2 == my_core,
        ((goal_exp // 2) ^ my_chip) * piece + clip * capacity + goal % capacity,
        -1,
    )
    place_t = place.transpose(0, 2, 1)
    gates_t = gates.transpose(0, 2, 1)

    all_weight = lax.all_gather(out_weight, "exp", axis=0, tiled=True)
    middle, normed = project(
        my_seq, merged, all_weight, residual.reshape(tok_count, model_width), norm_gain
    )
    mid_float = middle.astype(jnp.float32)

    def dispatch(hop, block, deps):
        pieces = to_slots(hop, chips, piece, place, block, trade(block), deps)
        return [over_chips(p, s) if s else p for s, p in enumerate(pieces)], pieces[0]

    def run(hop, deps):
        return expert(hop, arrived[hop], gate_mat, up_mat, down_mat, deps)

    def give_back(hop, partial, after_deps, deps):
        if after_deps:
            partial = after(partial, after_deps)
        returned = [over_chips(p, s) if s else p for s, p in enumerate(partial)]
        mine, other = combine(hop, returned, place_t, gates_t, deps)
        total = mine + over_cores(other).astype(jnp.float32)
        if hop == 0:
            return total, mine
        total = total.astype(jnp.bfloat16)
        half = tok_count // 2
        return [over_seq(total[:half], hop), over_seq(total[half:], hop)], total

    arrived = {}
    arrived[0], own0 = dispatch(0, normed, [])
    (normed_out,) = after([normed], [own0])
    blocks = [normed] + [over_seq(normed_out, hop) for hop in range(1, seq_count)]
    arrived[1], own1 = dispatch(1, blocks[1], arrived[0])
    done0 = run(0, [own1])
    arrived[2], own2 = dispatch(2, blocks[2], arrived[1] + [done0[0]])
    done1 = run(1, [own2])
    arrived[3], own3 = dispatch(3, blocks[3], arrived[2] + [done1[0]])
    done2 = run(2, [own3])
    done3 = run(3, [done2[0]])
    back2, mark2 = give_back(2, done2, [], [done3[0]])
    back3, mark3 = give_back(3, done3, [], [mark2, back2[0]])
    back1, mark1 = give_back(1, done1, [mark2], [mark3, back2[1], back3[0]])
    back0, _ = give_back(0, done0, [mark3], [mark1, back3[1]])
    result = mid_float + back0
    for back in (back1, back2, back3):
        result = result + jnp.concatenate(back, axis=0).astype(jnp.float32)
    return result.astype(jnp.bfloat16).reshape(1, tok_count, model_width)


def solution(mesh):
    placed = (
        P("exp", "seq", None),
        P("exp", "seq", None),
        P("exp", None),
        P(),
        P("exp", "seq", None),
        P("exp", "seq", None),
        P("exp", None, "seq"),
        P("exp", None, "seq"),
        P("exp", "seq", None),
    )
    return jax.shard_map(
        per_device, mesh=mesh, in_specs=placed, out_specs=P("exp", "seq", None), check_vma=False
    )
```

```python
import functools

import jax
import jax.numpy as jnp
from jax import lax
from jax.experimental import pallas as pl
from jax.experimental.pallas import tpu as pltpu
from jax.sharding import PartitionSpec as P

HEADS = 16
HEAD_DIM = 128
TOP = 2
TRADES = 2
AHEAD = 2
COVER = 16
PAIRS = [(0, 1), (1, 0), (2, 3), (3, 2)]
CROSS = [(1, 2), (2, 1)]
OUT = [(1, 0), (2, 3)]
IN = [(0, 1), (3, 2)]
FAR = [(1, 3), (2, 0)]
HID_TILE = 512
OUT_TILE = 1024
VMEM_LIMIT = 16 * 1024 * 1024
ANY = pl.BlockSpec(memory_space=pl.ANY)


def xor_pairs(count, offset):
    return [(i, i ^ offset) for i in range(count)]


def whole(shape):
    return pl.BlockSpec(shape, lambda *_: (0,) * len(shape))


def params():
    return pltpu.CompilerParams(vmem_limit_bytes=VMEM_LIMIT)


def cost(flops, bytes_accessed, transcendentals):
    return pl.CostEstimate(
        flops=flops, bytes_accessed=bytes_accessed, transcendentals=transcendentals
    )


def after(arrays, deps):
    count = len(arrays)
    return pl.pallas_call(
        lambda *_: None,
        in_specs=[ANY] * (count + len(deps)),
        out_specs=[ANY] * count,
        out_shape=[jax.ShapeDtypeStruct(a.shape, a.dtype) for a in arrays],
        input_output_aliases={i: i for i in range(count)},
        compiler_params=pltpu.CompilerParams(vmem_limit_bytes=1024 * 1024),
        cost_estimate=cost(0, 0, 0),
        name="after",
    )(*arrays, *deps)


def split_kernel(count, seq_ref, *refs):
    for i in range(count):
        refs[count + i][...] = refs[i][...]


def split_heads(my_seq, laid, count):
    tok, width = laid.shape
    cols = width // (3 * count)

    def source(hop):
        return pl.BlockSpec((tok, cols), lambda w, seq: (0, w * count + (seq[0] ^ hop)))

    return pl.pallas_call(
        functools.partial(split_kernel, count),
        grid_spec=pltpu.PrefetchScalarGridSpec(
            num_scalar_prefetch=1,
            grid=(3,),
            in_specs=[source(hop) for hop in range(count)],
            out_specs=[pl.BlockSpec((tok, cols), lambda w, seq: (0, w))] * count,
        ),
        out_shape=[jax.ShapeDtypeStruct((tok, 3 * cols), laid.dtype)] * count,
        compiler_params=params(),
        cost_estimate=cost(0, 4 * tok * width, 0),
        name="split_heads",
    )(my_seq.reshape(1), *([laid] * count))


def attend_kernel(count, *refs):
    parts, outs = refs[: 3 * count], refs[3 * count :]
    block = outs[0].shape[0]
    query, key, value = (
        jnp.concatenate([p[...] for p in parts[w * count : (w + 1) * count]], axis=0)
        for w in range(3)
    )
    scores = lax.dot_general(
        query, key, (((1,), (1,)), ((), ())), preferred_element_type=jnp.float32
    ) * HEAD_DIM ** (-0.5)
    top = jnp.max(scores, axis=-1, keepdims=True)
    grown = jnp.exp(scores - top)
    total = jnp.sum(grown, axis=-1, keepdims=True)
    mixed = jnp.dot(grown.astype(jnp.bfloat16), value, preferred_element_type=jnp.float32)
    mixed = (mixed / total).astype(jnp.bfloat16)
    for i in range(count):
        outs[i][...] = mixed[i * block : (i + 1) * block]


def attend(blocks, head_local):
    count = len(blocks)
    tok = blocks[0].shape[0]
    clip_len = count * tok

    def part(which):
        return pl.BlockSpec((tok, HEAD_DIM), lambda h: (0, which * head_local + h))

    return pl.pallas_call(
        functools.partial(attend_kernel, count),
        grid=(head_local,),
        in_specs=[part(which) for which in range(3) for _ in range(count)],
        out_specs=[pl.BlockSpec((tok, HEAD_DIM), lambda h: (0, h))] * count,
        out_shape=[jax.ShapeDtypeStruct((tok, head_local * HEAD_DIM), jnp.bfloat16)] * count,
        compiler_params=params(),
        cost_estimate=cost(
            4 * head_local * clip_len * clip_len * HEAD_DIM,
            8 * clip_len * head_local * HEAD_DIM,
            head_local * clip_len * clip_len,
        ),
        name="attend",
    )(*(list(blocks) * 3))


def project_kernel(count, seq_ref, *refs):
    parts = refs[:count]
    weight_ref, res_ref, gain_ref, mid_ref, norm_ref, acc_ref = refs[count:]
    step = pl.program_id(0)
    for i in range(count):

        @pl.when(step == i)
        def _(i=i):
            term = jnp.dot(parts[i][...], weight_ref[...], preferred_element_type=jnp.float32)
            acc_ref[...] = (res_ref[...].astype(jnp.float32) if i == 0 else acc_ref[...]) + term

    @pl.when(step == count - 1)
    def _():
        middle = acc_ref[...].astype(jnp.bfloat16)
        mid_ref[...] = middle
        mid_float = middle.astype(jnp.float32)
        mean = jnp.mean(mid_float * mid_float, axis=-1, keepdims=True)
        norm_ref[...] = (mid_float * lax.rsqrt(mean + 1e-06) * gain_ref[...]).astype(
            jnp.bfloat16
        )


def project(my_seq, parts, weight, residual, gain):
    count = len(parts)
    tok, depth = parts[0].shape
    width = weight.shape[1]
    out = jax.ShapeDtypeStruct((tok, width), jnp.bfloat16)
    return pl.pallas_call(
        functools.partial(project_kernel, count),
        grid_spec=pltpu.PrefetchScalarGridSpec(
            num_scalar_prefetch=1,
            grid=(count,),
            in_specs=[whole((tok, depth))] * count
            + [
                pl.BlockSpec((depth, width), lambda k, seq: (seq[0] ^ k, 0)),
                whole((tok, width)),
                whole((1, width)),
            ],
            out_specs=[whole((tok, width))] * 2,
            scratch_shapes=[pltpu.VMEM((tok, width), jnp.float32)],
        ),
        out_shape=[out, out],
        compiler_params=params(),
        cost_estimate=cost(2 * tok * count * depth * width, 2 * count * depth * width, 0),
        name="project",
    )(
        my_seq.reshape(1),
        *parts,
        pltpu.with_memory_space_constraint(weight, pltpu.HBM),
        residual,
        gain.reshape(1, width),
    )


def slot_kernel(hop, chips, place_ref, mine_ref, *rest):
    outs = rest[-chips:]
    piece = outs[0].shape[0]
    place = place_ref[hop]
    row = lax.broadcasted_iota(jnp.int32, (chips * piece, place.shape[-1]), 0)
    others = rest[:TRADES]
    halves = []
    for which in range(2):
        hit = (row == place[2 * which : 2 * which + 1]) | (
            row == place[2 * which + 1 : 2 * which + 2]
        )
        halves.append(jnp.where(hit, 1.0, 0.0).astype(jnp.bfloat16))
    slotted = jnp.dot(
        jnp.concatenate(halves, axis=1),
        jnp.concatenate([mine_ref[...]] + [o[...] for o in others], axis=0),
        preferred_element_type=jnp.float32,
    ).astype(jnp.bfloat16)
    for step in range(chips):
        outs[step][...] = slotted[step * piece : (step + 1) * piece]


def to_slots(hop, chips, piece, place, mine, others, deps):
    tok, width = mine.shape
    return pl.pallas_call(
        functools.partial(slot_kernel, hop, chips),
        in_specs=[whole(place.shape), whole(mine.shape)]
        + [whole(o.shape) for o in others]
        + [ANY] * len(deps),
        out_specs=[whole((piece, width))] * chips,
        out_shape=[jax.ShapeDtypeStruct((piece, width), jnp.bfloat16)] * chips,
        compiler_params=params(),
        cost_estimate=cost(4 * chips * piece * tok * width, 2 * width * (2 * tok + chips * piece), 0),
        name=f"slots{hop}",
    )(place, mine, *others, *deps)


def expert_kernel(chips, n_deps, *refs):
    pieces = refs[:chips]
    gate_hbm, up_hbm, down_hbm = refs[chips : chips + 3]
    outs = refs[chips + 3 + n_deps : 2 * chips + 3 + n_deps]
    rows_ref, hid_ref, gate_ref, up_ref, down_ref, sem = refs[-6:]
    piece = pieces[0].shape[0]
    hid, width = down_ref.shape
    hid_tiles = [slice(at, min(at + HID_TILE, hid)) for at in range(0, hid, HID_TILE)]
    out_tiles = [slice(at, at + OUT_TILE) for at in range(0, width, OUT_TILE)]
    stages = [[(gate_hbm, gate_ref, t), (up_hbm, up_ref, t)] for t in hid_tiles]
    stages += [[(down_hbm, down_ref, t)] for t in out_tiles]
    copies, count = [], 0
    for stage in stages:
        group = []
        for source, target, tile in stage:
            group.append(
                pltpu.make_async_copy(source.at[:, tile], target.at[:, tile], sem.at[count])
            )
            count += 1
        copies.append(group)

    def start(n):
        if n < len(copies):
            for copy in copies[n]:
                copy.start()

    def wait(n):
        for copy in copies[n]:
            copy.wait()
        start(n + AHEAD)

    for n in range(AHEAD):
        start(n)
    for i in range(chips):
        rows_ref[i * piece : (i + 1) * piece, :] = pieces[i][...]
    for n, tile in enumerate(hid_tiles):
        wait(n)
        gate_val = jnp.dot(rows_ref[...], gate_ref[:, tile], preferred_element_type=jnp.float32)
        up_val = jnp.dot(rows_ref[...], up_ref[:, tile], preferred_element_type=jnp.float32)
        hidden = gate_val / (1.0 + jnp.exp(-gate_val)) * up_val
        hid_ref[:, tile] = hidden.astype(jnp.bfloat16)
    for n, tile in enumerate(out_tiles):
        wait(len(hid_tiles) + n)
        out = jnp.dot(hid_ref[...], down_ref[:, tile], preferred_element_type=jnp.float32)
        out = out.astype(jnp.bfloat16)
        for i in range(chips):
            outs[i][:, tile] = out[i * piece : (i + 1) * piece]


def expert(hop, pieces, gate_mat, up_mat, down_mat, deps):
    chips = len(pieces)
    piece, width = pieces[0].shape
    hid = gate_mat.shape[-1]
    rows = chips * piece
    in_vmem = pl.BlockSpec(memory_space=pltpu.VMEM)
    in_hbm = pl.BlockSpec(memory_space=pltpu.HBM)
    n_sems = 2 * -(-hid // HID_TILE) + width // OUT_TILE
    return pl.pallas_call(
        functools.partial(expert_kernel, chips, len(deps)),
        in_specs=[in_vmem] * chips + [in_hbm] * 3 + [ANY] * len(deps),
        out_specs=[in_vmem] * chips,
        out_shape=[jax.ShapeDtypeStruct((piece, width), jnp.bfloat16)] * chips,
        scratch_shapes=[
            pltpu.VMEM((rows, width), jnp.bfloat16),
            pltpu.VMEM((rows, hid), jnp.bfloat16),
            pltpu.VMEM((width, hid), jnp.bfloat16),
            pltpu.VMEM((width, hid), jnp.bfloat16),
            pltpu.VMEM((hid, width), jnp.bfloat16),
            pltpu.SemaphoreType.DMA((n_sems,)),
        ],
        compiler_params=pltpu.CompilerParams(vmem_limit_bytes=32 * 1024 * 1024),
        cost_estimate=cost(6 * rows * width * hid, 6 * width * hid, rows * hid),
        name=f"expert{hop}",
    )(
        *pieces,
        *(pltpu.with_memory_space_constraint(w, pltpu.HBM) for w in (gate_mat, up_mat, down_mat)),
        *deps,
    )


def combine_kernel(hop, chips, n_deps, place_ref, gates_ref, *refs):
    pieces = refs[:chips]
    mine_ref, other_ref = refs[chips + n_deps :]
    rows = jnp.concatenate([p[...] for p in pieces], axis=0)
    place = place_ref[hop]
    gates = gates_ref[hop]
    column = lax.broadcasted_iota(jnp.int32, (place.shape[0], rows.shape[0]), 1)
    for which, out_ref in ((0, mine_ref), (1, other_ref)):
        total = 0.0
        for choice in range(TOP):
            at = 2 * which + choice
            picking = jnp.where(column == place[:, at : at + 1], 1.0, 0.0).astype(jnp.bfloat16)
            picked = jnp.dot(picking, rows, preferred_element_type=jnp.float32)
            total = total + picked * gates[:, at : at + 1]
        out_ref[...] = total.astype(out_ref.dtype)


def combine(hop, pieces, place, gates, deps):
    chips = len(pieces)
    piece, width = pieces[0].shape
    tok = place.shape[1]
    tile = pl.BlockSpec((tok, OUT_TILE), lambda i: (0, i))
    return pl.pallas_call(
        functools.partial(combine_kernel, hop, chips, len(deps)),
        grid=(width // OUT_TILE,),
        in_specs=[whole(place.shape), whole(gates.shape)]
        + [pl.BlockSpec((piece, OUT_TILE), lambda i: (0, i))] * chips
        + [ANY] * len(deps),
        out_specs=[tile, tile],
        out_shape=[
            jax.ShapeDtypeStruct((tok, width), jnp.float32),
            jax.ShapeDtypeStruct((tok, width), jnp.bfloat16),
        ],
        compiler_params=params(),
        cost_estimate=cost(COVER * 8 * tok * chips * piece * width, COVER * 2 * width * (chips * piece + 3 * tok), 0),
        name=f"combine{hop}",
    )(place, gates, *pieces, *deps)


def per_device(
    attn_inputs,
    residual,
    out_weight,
    norm_gain,
    expert_ids,
    gate_weights,
    gate_weight,
    up_weight,
    down_weight,
):
    tok_count = attn_inputs.shape[1]
    seq_count = lax.axis_size("seq")
    expert_count = lax.axis_size("exp")
    chips = expert_count // 2
    my_seq = lax.axis_index("seq")
    my_exp = lax.axis_index("exp")
    my_core, my_chip = my_exp % 2, my_exp // 2
    model_width = residual.shape[-1]
    head_local = HEADS // seq_count
    capacity = 5 * tok_count // (2 * expert_count)
    piece = -(-2 * capacity // 16) * 16

    def over_seq(value, hop):
        return lax.ppermute(value, "seq", xor_pairs(seq_count, hop))

    def over_chips(value, step):
        return lax.ppermute(value, "exp", xor_pairs(expert_count, 2 * step))

    def over_cores(value):
        return lax.ppermute(value, "exp", xor_pairs(expert_count, 1))

    gate_mat, up_mat, down_mat = gate_weight[0], up_weight[0], down_weight[0]

    def trade(value):
        part = value.shape[0] // TRADES
        return [over_cores(value[i * part : (i + 1) * part]) for i in range(TRADES)]

    blocks = split_heads(my_seq, attn_inputs.reshape(tok_count, 3 * HEADS * HEAD_DIM), seq_count)
    blocks = [over_seq(part, hop) if hop else part for hop, part in enumerate(blocks)]
    attended = attend(blocks, head_local)
    merged = [over_seq(p, hop) if hop else p for hop, p in enumerate(attended)]

    route_ids = expert_ids.reshape(tok_count * TOP)
    one_hot = (
        route_ids[:, None] == jnp.arange(expert_count, dtype=jnp.int32)[None, :]
    ).astype(jnp.int32)
    before = jnp.cumsum(one_hot, axis=0) - one_hot
    slot_ids = jnp.sum(before * one_hot, axis=-1)
    target = (route_ids * capacity + slot_ids).reshape(tok_count, TOP)
    route = jnp.concatenate([target.astype(jnp.float32), gate_weights[0]], axis=1).T
    (route_out,) = after([route], [blocks[1]])
    routes = [route] + [over_seq(route_out, hop) for hop in range(1, seq_count)]
    in_middle = (my_seq == 1) | (my_seq == 2)
    route = jnp.stack(
        [
            routes[0],
            routes[1],
            jnp.where(in_middle, routes[3], routes[2]),
            jnp.where(in_middle, routes[2], routes[3]),
        ]
    )
    both = jnp.concatenate([route, over_cores(route)], axis=1)
    goal = jnp.concatenate([both[:, :TOP], both[:, 2 * TOP : 3 * TOP]], axis=1).astype(jnp.int32)
    gates = jnp.concatenate([both[:, TOP : 2 * TOP], both[:, 3 * TOP :]], axis=1)
    goal_exp = goal // capacity
    clip = (jnp.arange(2 * TOP, dtype=jnp.int32) // TOP)[None, :, None]
    place = jnp.where(
        goal_exp % 2 == my_core,
        ((goal_exp // 2) ^ my_chip) * piece + clip * capacity + goal % capacity,
        -1,
    )
    place_t = place.transpose(0, 2, 1)
    gates_t = gates.transpose(0, 2, 1)

    all_weight = lax.all_gather(out_weight, "exp", axis=0, tiled=True)
    middle, normed = project(
        my_seq, merged, all_weight, residual.reshape(tok_count, model_width), norm_gain
    )
    mid_float = middle.astype(jnp.float32)

    def dispatch(hop, block, deps):
        pieces = to_slots(hop, chips, piece, place, block, trade(block), deps)
        return [over_chips(p, s) if s else p for s, p in enumerate(pieces)], pieces[0]

    def run(hop, deps):
        return expert(hop, arrived[hop], gate_mat, up_mat, down_mat, deps)

    def give_back(hop, partial, after_deps, deps):
        if after_deps:
            partial = after(partial, after_deps)
        returned = [over_chips(p, s) if s else p for s, p in enumerate(partial)]
        mine, other = combine(hop, returned, place_t, gates_t, deps)
        total = mine + over_cores(other).astype(jnp.float32)
        return total, total.astype(jnp.bfloat16)

    def hop_along(value, pairs):
        return lax.ppermute(value, "seq", pairs)

    arrived = {}
    arrived[0], own0 = dispatch(0, normed, [])
    (normed_out,) = after([normed], [own0])
    pair_block = hop_along(normed_out, PAIRS)
    cross_block = hop_along(normed_out, CROSS)
    cross_pair = hop_along(pair_block, CROSS)
    arrived[1], own1 = dispatch(1, pair_block, arrived[0])
    done0 = run(0, [own1])
    (kept,) = after([cross_block], [done0[0]])
    second = jnp.where(in_middle, kept, hop_along(cross_block, OUT))
    arrived[2], own2 = dispatch(2, second, [done0[0]])
    done1 = run(1, [own2])
    (kept,) = after([cross_pair], [done1[0]])
    third = jnp.where(in_middle, kept, hop_along(cross_pair, OUT))
    arrived[3], own3 = dispatch(3, third, [done1[0]])
    done2 = run(2, [own3])
    done3 = run(3, [done2[0]])
    total2, send2 = give_back(2, done2, [], [done3[0]])
    in2 = hop_along(send2, IN)
    total3, send3 = give_back(3, done3, [], [send2])
    in3 = hop_along(send3, IN)
    send2 = (total2 + in2.astype(jnp.float32)).astype(jnp.bfloat16)
    back2 = hop_along(send2, CROSS)
    total1, send1 = give_back(1, done1, [], [send3, send2])
    back1 = hop_along(send1, PAIRS)
    send3 = (total3 + in3.astype(jnp.float32)).astype(jnp.bfloat16)
    back3 = hop_along(send3, FAR)
    result, _ = give_back(0, done0, [], [back1, back2, back3])
    result = mid_float + result
    for back in (back1, back2, back3):
        result = result + back.astype(jnp.float32)
    return result.astype(jnp.bfloat16).reshape(1, tok_count, model_width)


def solution(mesh):
    placed = (
        P("exp", "seq", None),
        P("exp", "seq", None),
        P("exp", None),
        P(),
        P("exp", "seq", None),
        P("exp", "seq", None),
        P("exp", None, "seq"),
        P("exp", None, "seq"),
        P("exp", "seq", None),
    )
    return jax.shard_map(
        per_device, mesh=mesh, in_specs=placed, out_specs=P("exp", "seq", None), check_vma=False
    )
```

```python
import functools

import jax
import jax.numpy as jnp
from jax import lax
from jax.experimental import pallas as pl
from jax.experimental.pallas import tpu as pltpu
from jax.sharding import PartitionSpec as P

HEADS = 16
HEAD_DIM = 128
TOP = 2
TRADES = 2
AHEAD = 2
COVER = 16
PAIRS = [(0, 1), (1, 0), (2, 3), (3, 2)]
CROSS = [(1, 2), (2, 1)]
OUT = [(1, 0), (2, 3)]
IN = [(0, 1), (3, 2)]
FAR = [(1, 3), (2, 0)]
HID_TILE = 512
OUT_TILE = 1024
VMEM_LIMIT = 16 * 1024 * 1024
ANY = pl.BlockSpec(memory_space=pl.ANY)


def xor_pairs(count, offset):
    return [(i, i ^ offset) for i in range(count)]


def whole(shape):
    return pl.BlockSpec(shape, lambda *_: (0,) * len(shape))


def params():
    return pltpu.CompilerParams(vmem_limit_bytes=VMEM_LIMIT)


def cost(flops, bytes_accessed, transcendentals):
    return pl.CostEstimate(
        flops=flops, bytes_accessed=bytes_accessed, transcendentals=transcendentals
    )


def after(arrays, deps):
    count = len(arrays)
    return pl.pallas_call(
        lambda *_: None,
        in_specs=[ANY] * (count + len(deps)),
        out_specs=[ANY] * count,
        out_shape=[jax.ShapeDtypeStruct(a.shape, a.dtype) for a in arrays],
        input_output_aliases={i: i for i in range(count)},
        compiler_params=pltpu.CompilerParams(vmem_limit_bytes=1024 * 1024),
        cost_estimate=cost(0, 0, 0),
        name="after",
    )(*arrays, *deps)


def split_kernel(count, seq_ref, *refs):
    for i in range(count):
        refs[count + i][...] = refs[i][...]


def split_heads(my_seq, laid, count):
    tok, width = laid.shape
    cols = width // (3 * count)

    def source(hop):
        return pl.BlockSpec((tok, cols), lambda w, seq: (0, w * count + (seq[0] ^ hop)))

    return pl.pallas_call(
        functools.partial(split_kernel, count),
        grid_spec=pltpu.PrefetchScalarGridSpec(
            num_scalar_prefetch=1,
            grid=(3,),
            in_specs=[source(hop) for hop in range(count)],
            out_specs=[pl.BlockSpec((tok, cols), lambda w, seq: (0, w))] * count,
        ),
        out_shape=[jax.ShapeDtypeStruct((tok, 3 * cols), laid.dtype)] * count,
        compiler_params=params(),
        cost_estimate=cost(0, 4 * tok * width, 0),
        name="split_heads",
    )(my_seq.reshape(1), *([laid] * count))


def attend_kernel(count, *refs):
    parts, outs = refs[: 3 * count], refs[3 * count :]
    block = outs[0].shape[0]
    query, key, value = (
        jnp.concatenate([p[...] for p in parts[w * count : (w + 1) * count]], axis=0)
        for w in range(3)
    )
    scores = lax.dot_general(
        query, key, (((1,), (1,)), ((), ())), preferred_element_type=jnp.float32
    ) * HEAD_DIM ** (-0.5)
    top = jnp.max(scores, axis=-1, keepdims=True)
    grown = jnp.exp(scores - top)
    total = jnp.sum(grown, axis=-1, keepdims=True)
    mixed = jnp.dot(grown.astype(jnp.bfloat16), value, preferred_element_type=jnp.float32)
    mixed = (mixed / total).astype(jnp.bfloat16)
    for i in range(count):
        outs[i][...] = mixed[i * block : (i + 1) * block]


def attend(blocks, head_local):
    count = len(blocks)
    tok = blocks[0].shape[0]
    clip_len = count * tok

    def part(which):
        return pl.BlockSpec((tok, HEAD_DIM), lambda h: (0, which * head_local + h))

    return pl.pallas_call(
        functools.partial(attend_kernel, count),
        grid=(head_local,),
        in_specs=[part(which) for which in range(3) for _ in range(count)],
        out_specs=[pl.BlockSpec((tok, HEAD_DIM), lambda h: (0, h))] * count,
        out_shape=[jax.ShapeDtypeStruct((tok, head_local * HEAD_DIM), jnp.bfloat16)] * count,
        compiler_params=params(),
        cost_estimate=cost(
            4 * head_local * clip_len * clip_len * HEAD_DIM,
            8 * clip_len * head_local * HEAD_DIM,
            head_local * clip_len * clip_len,
        ),
        name="attend",
    )(*(list(blocks) * 3))


def project_kernel(count, seq_ref, *refs):
    parts = refs[:count]
    weight_ref, res_ref, gain_ref, mid_ref, norm_ref, acc_ref = refs[count:]
    step = pl.program_id(0)
    for i in range(count):

        @pl.when(step == i)
        def _(i=i):
            term = jnp.dot(parts[i][...], weight_ref[...], preferred_element_type=jnp.float32)
            acc_ref[...] = (res_ref[...].astype(jnp.float32) if i == 0 else acc_ref[...]) + term

    @pl.when(step == count - 1)
    def _():
        middle = acc_ref[...].astype(jnp.bfloat16)
        mid_ref[...] = middle
        mid_float = middle.astype(jnp.float32)
        mean = jnp.mean(mid_float * mid_float, axis=-1, keepdims=True)
        norm_ref[...] = (mid_float * lax.rsqrt(mean + 1e-06) * gain_ref[...]).astype(
            jnp.bfloat16
        )


def project(my_seq, parts, weight, residual, gain):
    count = len(parts)
    tok, depth = parts[0].shape
    width = weight.shape[1]
    out = jax.ShapeDtypeStruct((tok, width), jnp.bfloat16)
    return pl.pallas_call(
        functools.partial(project_kernel, count),
        grid_spec=pltpu.PrefetchScalarGridSpec(
            num_scalar_prefetch=1,
            grid=(count,),
            in_specs=[whole((tok, depth))] * count
            + [
                pl.BlockSpec((depth, width), lambda k, seq: (seq[0] ^ k, 0)),
                whole((tok, width)),
                whole((1, width)),
            ],
            out_specs=[whole((tok, width))] * 2,
            scratch_shapes=[pltpu.VMEM((tok, width), jnp.float32)],
        ),
        out_shape=[out, out],
        compiler_params=params(),
        cost_estimate=cost(2 * tok * count * depth * width, 2 * count * depth * width, 0),
        name="project",
    )(
        my_seq.reshape(1),
        *parts,
        pltpu.with_memory_space_constraint(weight, pltpu.HBM),
        residual,
        gain.reshape(1, width),
    )


def slot_kernel(hop, chips, place_ref, mine_ref, *rest):
    outs = rest[-chips:]
    piece = outs[0].shape[0]
    place = place_ref[hop]
    row = lax.broadcasted_iota(jnp.int32, (chips * piece, place.shape[-1]), 0)
    others = rest[:TRADES]
    halves = []
    for which in range(2):
        hit = (row == place[2 * which : 2 * which + 1]) | (
            row == place[2 * which + 1 : 2 * which + 2]
        )
        halves.append(jnp.where(hit, 1.0, 0.0).astype(jnp.bfloat16))
    slotted = jnp.dot(
        jnp.concatenate(halves, axis=1),
        jnp.concatenate([mine_ref[...]] + [o[...] for o in others], axis=0),
        preferred_element_type=jnp.float32,
    ).astype(jnp.bfloat16)
    for step in range(chips):
        outs[step][...] = slotted[step * piece : (step + 1) * piece]


def to_slots(hop, chips, piece, place, mine, others, deps):
    tok, width = mine.shape
    return pl.pallas_call(
        functools.partial(slot_kernel, hop, chips),
        in_specs=[whole(place.shape), whole(mine.shape)]
        + [whole(o.shape) for o in others]
        + [ANY] * len(deps),
        out_specs=[whole((piece, width))] * chips,
        out_shape=[jax.ShapeDtypeStruct((piece, width), jnp.bfloat16)] * chips,
        compiler_params=params(),
        cost_estimate=cost(4 * chips * piece * tok * width, 2 * width * (2 * tok + chips * piece), 0),
        name=f"slots{hop}",
    )(place, mine, *others, *deps)


def expert_kernel(chips, n_deps, *refs):
    pieces = refs[:chips]
    gate_hbm, up_hbm, down_hbm = refs[chips : chips + 3]
    outs = refs[chips + 3 + n_deps : 2 * chips + 3 + n_deps]
    rows_ref, hid_ref, gate_ref, up_ref, down_ref, sem = refs[-6:]
    piece = pieces[0].shape[0]
    hid, width = down_ref.shape
    hid_tiles = [slice(at, min(at + HID_TILE, hid)) for at in range(0, hid, HID_TILE)]
    out_tiles = [slice(at, at + OUT_TILE) for at in range(0, width, OUT_TILE)]
    stages = [[(gate_hbm, gate_ref, t), (up_hbm, up_ref, t)] for t in hid_tiles]
    stages += [[(down_hbm, down_ref, t)] for t in out_tiles]
    copies, count = [], 0
    for stage in stages:
        group = []
        for source, target, tile in stage:
            group.append(
                pltpu.make_async_copy(source.at[:, tile], target.at[:, tile], sem.at[count])
            )
            count += 1
        copies.append(group)

    def start(n):
        if n < len(copies):
            for copy in copies[n]:
                copy.start()

    def wait(n):
        for copy in copies[n]:
            copy.wait()
        start(n + AHEAD)

    for n in range(AHEAD):
        start(n)
    for i in range(chips):
        rows_ref[i * piece : (i + 1) * piece, :] = pieces[i][...]
    for n, tile in enumerate(hid_tiles):
        wait(n)
        gate_val = jnp.dot(rows_ref[...], gate_ref[:, tile], preferred_element_type=jnp.float32)
        up_val = jnp.dot(rows_ref[...], up_ref[:, tile], preferred_element_type=jnp.float32)
        hidden = gate_val / (1.0 + jnp.exp(-gate_val)) * up_val
        hid_ref[:, tile] = hidden.astype(jnp.bfloat16)
    for n, tile in enumerate(out_tiles):
        wait(len(hid_tiles) + n)
        out = jnp.dot(hid_ref[...], down_ref[:, tile], preferred_element_type=jnp.float32)
        out = out.astype(jnp.bfloat16)
        for i in range(chips):
            outs[i][:, tile] = out[i * piece : (i + 1) * piece]


def expert(hop, pieces, gate_mat, up_mat, down_mat, deps):
    chips = len(pieces)
    piece, width = pieces[0].shape
    hid = gate_mat.shape[-1]
    rows = chips * piece
    in_vmem = pl.BlockSpec(memory_space=pltpu.VMEM)
    in_hbm = pl.BlockSpec(memory_space=pltpu.HBM)
    n_sems = 2 * -(-hid // HID_TILE) + width // OUT_TILE
    return pl.pallas_call(
        functools.partial(expert_kernel, chips, len(deps)),
        in_specs=[in_vmem] * chips + [in_hbm] * 3 + [ANY] * len(deps),
        out_specs=[in_vmem] * chips,
        out_shape=[jax.ShapeDtypeStruct((piece, width), jnp.bfloat16)] * chips,
        scratch_shapes=[
            pltpu.VMEM((rows, width), jnp.bfloat16),
            pltpu.VMEM((rows, hid), jnp.bfloat16),
            pltpu.VMEM((width, hid), jnp.bfloat16),
            pltpu.VMEM((width, hid), jnp.bfloat16),
            pltpu.VMEM((hid, width), jnp.bfloat16),
            pltpu.SemaphoreType.DMA((n_sems,)),
        ],
        compiler_params=pltpu.CompilerParams(vmem_limit_bytes=32 * 1024 * 1024),
        cost_estimate=cost(6 * rows * width * hid, 6 * width * hid, rows * hid),
        name=f"expert{hop}",
    )(
        *pieces,
        *(pltpu.with_memory_space_constraint(w, pltpu.HBM) for w in (gate_mat, up_mat, down_mat)),
        *deps,
    )


def combine_kernel(hop, chips, n_deps, place_ref, gates_ref, *refs):
    pieces = refs[:chips]
    mine_ref, other_ref = refs[chips + n_deps :]
    rows = jnp.concatenate([p[...] for p in pieces], axis=0)
    place = place_ref[hop]
    gates = gates_ref[hop]
    column = lax.broadcasted_iota(jnp.int32, (place.shape[0], rows.shape[0]), 1)
    for which, out_ref in ((0, mine_ref), (1, other_ref)):
        total = 0.0
        for choice in range(TOP):
            at = 2 * which + choice
            picking = jnp.where(column == place[:, at : at + 1], 1.0, 0.0).astype(jnp.bfloat16)
            picked = jnp.dot(picking, rows, preferred_element_type=jnp.float32)
            total = total + picked * gates[:, at : at + 1]
        out_ref[...] = total.astype(out_ref.dtype)


def combine(hop, pieces, place, gates, deps):
    chips = len(pieces)
    piece, width = pieces[0].shape
    tok = place.shape[1]
    tile = pl.BlockSpec((tok, OUT_TILE), lambda i: (0, i))
    return pl.pallas_call(
        functools.partial(combine_kernel, hop, chips, len(deps)),
        grid=(width // OUT_TILE,),
        in_specs=[whole(place.shape), whole(gates.shape)]
        + [pl.BlockSpec((piece, OUT_TILE), lambda i: (0, i))] * chips
        + [ANY] * len(deps),
        out_specs=[tile, tile],
        out_shape=[
            jax.ShapeDtypeStruct((tok, width), jnp.float32),
            jax.ShapeDtypeStruct((tok, width), jnp.bfloat16),
        ],
        compiler_params=params(),
        cost_estimate=cost(COVER * 8 * tok * chips * piece * width, COVER * 2 * width * (chips * piece + 3 * tok), 0),
        name=f"combine{hop}",
    )(place, gates, *pieces, *deps)


def per_device(
    attn_inputs,
    residual,
    out_weight,
    norm_gain,
    expert_ids,
    gate_weights,
    gate_weight,
    up_weight,
    down_weight,
):
    tok_count = attn_inputs.shape[1]
    seq_count = lax.axis_size("seq")
    expert_count = lax.axis_size("exp")
    chips = expert_count // 2
    my_seq = lax.axis_index("seq")
    my_exp = lax.axis_index("exp")
    my_core, my_chip = my_exp % 2, my_exp // 2
    model_width = residual.shape[-1]
    head_local = HEADS // seq_count
    capacity = 5 * tok_count // (2 * expert_count)
    piece = -(-2 * capacity // 16) * 16

    def over_seq(value, hop):
        return lax.ppermute(value, "seq", xor_pairs(seq_count, hop))

    def over_chips(value, step):
        return lax.ppermute(value, "exp", xor_pairs(expert_count, 2 * step))

    def over_cores(value):
        return lax.ppermute(value, "exp", xor_pairs(expert_count, 1))

    gate_mat, up_mat, down_mat = gate_weight[0], up_weight[0], down_weight[0]

    def trade(value):
        part = value.shape[0] // TRADES
        return [over_cores(value[i * part : (i + 1) * part]) for i in range(TRADES)]

    blocks = split_heads(my_seq, attn_inputs.reshape(tok_count, 3 * HEADS * HEAD_DIM), seq_count)
    blocks = [over_seq(part, hop) if hop else part for hop, part in enumerate(blocks)]
    attended = attend(blocks, head_local)
    merged = [over_seq(p, hop) if hop else p for hop, p in enumerate(attended)]

    route_ids = expert_ids.reshape(tok_count * TOP)
    one_hot = (
        route_ids[:, None] == jnp.arange(expert_count, dtype=jnp.int32)[None, :]
    ).astype(jnp.int32)
    before = jnp.cumsum(one_hot, axis=0) - one_hot
    slot_ids = jnp.sum(before * one_hot, axis=-1)
    target = (route_ids * capacity + slot_ids).reshape(tok_count, TOP)
    route = jnp.concatenate([target.astype(jnp.float32), gate_weights[0]], axis=1).T
    (route_out,) = after([route], [blocks[1]])
    routes = [route] + [over_seq(route_out, hop) for hop in range(1, seq_count)]
    in_middle = (my_seq == 1) | (my_seq == 2)
    route = jnp.stack(
        [
            routes[0],
            routes[1],
            jnp.where(in_middle, routes[3], routes[2]),
            jnp.where(in_middle, routes[2], routes[3]),
        ]
    )
    both = jnp.concatenate([route, over_cores(route)], axis=1)
    goal = jnp.concatenate([both[:, :TOP], both[:, 2 * TOP : 3 * TOP]], axis=1).astype(jnp.int32)
    gates = jnp.concatenate([both[:, TOP : 2 * TOP], both[:, 3 * TOP :]], axis=1)
    goal_exp = goal // capacity
    clip = (jnp.arange(2 * TOP, dtype=jnp.int32) // TOP)[None, :, None]
    place = jnp.where(
        goal_exp % 2 == my_core,
        ((goal_exp // 2) ^ my_chip) * piece + clip * capacity + goal % capacity,
        -1,
    )
    place_t = place.transpose(0, 2, 1)
    gates_t = gates.transpose(0, 2, 1)

    all_weight = lax.all_gather(out_weight, "exp", axis=0, tiled=True)
    middle, normed = project(
        my_seq, merged, all_weight, residual.reshape(tok_count, model_width), norm_gain
    )
    mid_float = middle.astype(jnp.float32)

    def dispatch(hop, block, deps):
        pieces = to_slots(hop, chips, piece, place, block, trade(block), deps)
        return [over_chips(p, s) if s else p for s, p in enumerate(pieces)], pieces[0]

    def run(hop, deps):
        return expert(hop, arrived[hop], gate_mat, up_mat, down_mat, deps)

    def give_back(hop, partial, after_deps, deps):
        if after_deps:
            partial = after(partial, after_deps)
        returned = [over_chips(p, s) if s else p for s, p in enumerate(partial)]
        mine, other = combine(hop, returned, place_t, gates_t, deps)
        total = mine + over_cores(other).astype(jnp.float32)
        return total, total.astype(jnp.bfloat16)

    def joined(total, received):
        return (total + received.astype(jnp.float32)).astype(jnp.bfloat16)

    def hop_along(value, pairs):
        return lax.ppermute(value, "seq", pairs)

    arrived = {}
    arrived[0], own0 = dispatch(0, normed, [])
    (normed_out,) = after([normed], [own0])
    pair_block = hop_along(normed_out, PAIRS)
    cross_block = hop_along(normed_out, CROSS)
    cross_pair = hop_along(pair_block, CROSS)
    arrived[1], own1 = dispatch(1, pair_block, arrived[0][1:2])
    done0 = run(0, [own1])
    (kept,) = after([cross_block], [done0[0]])
    second = jnp.where(in_middle, kept, hop_along(cross_block, OUT))
    arrived[2], own2 = dispatch(2, second, [done0[0]])
    done1 = run(1, [own2])
    (kept,) = after([cross_pair], [done1[0]])
    third = jnp.where(in_middle, kept, hop_along(cross_pair, OUT))
    arrived[3], own3 = dispatch(3, third, [done1[0]])
    done2 = run(2, [own3])
    done3 = run(3, [done2[0]])
    total2, send2 = give_back(2, done2, [], [done3[0]])
    in2 = hop_along(send2, IN)
    next2 = joined(total2, in2)
    back2 = hop_along(next2, CROSS)
    total3, send3 = give_back(3, done3, [], [send2])
    in3 = hop_along(send3, IN)
    next3 = joined(total3, in3)
    back3 = hop_along(next3, FAR)
    total1, send1 = give_back(1, done1, [], [send3, next2])
    back1 = hop_along(send1, PAIRS)
    result, _ = give_back(0, done0, [], [send1])
    result = mid_float + result
    for back in (back1, back2, back3):
        result = result + back.astype(jnp.float32)
    return result.astype(jnp.bfloat16).reshape(1, tok_count, model_width)


def solution(mesh):
    placed = (
        P("exp", "seq", None),
        P("exp", "seq", None),
        P("exp", None),
        P(),
        P("exp", "seq", None),
        P("exp", "seq", None),
        P("exp", None, "seq"),
        P("exp", None, "seq"),
        P("exp", "seq", None),
    )
    return jax.shard_map(
        per_device, mesh=mesh, in_specs=placed, out_specs=P("exp", "seq", None), check_vma=False
    )
```

```python
import functools

import jax
import jax.numpy as jnp
from jax import lax
from jax.experimental import pallas as pl
from jax.experimental.pallas import tpu as pltpu
from jax.sharding import PartitionSpec as P

HEADS = 16
HEAD_DIM = 128
TOP = 2
TRADES = 2
AHEAD = 2
COVER = 16
PAIRS = [(0, 1), (1, 0), (2, 3), (3, 2)]
CROSS = [(1, 2), (2, 1)]
OUT = [(1, 0), (2, 3)]
IN = [(0, 1), (3, 2)]
FAR = [(1, 3), (2, 0)]
HID_TILE = 512
OUT_TILE = 1024
VMEM_LIMIT = 16 * 1024 * 1024
ANY = pl.BlockSpec(memory_space=pl.ANY)


def xor_pairs(count, offset):
    return [(i, i ^ offset) for i in range(count)]


def whole(shape):
    return pl.BlockSpec(shape, lambda *_: (0,) * len(shape))


def params():
    return pltpu.CompilerParams(vmem_limit_bytes=VMEM_LIMIT)


def cost(flops, bytes_accessed, transcendentals):
    return pl.CostEstimate(
        flops=flops, bytes_accessed=bytes_accessed, transcendentals=transcendentals
    )


def after(arrays, deps):
    count = len(arrays)
    return pl.pallas_call(
        lambda *_: None,
        in_specs=[ANY] * (count + len(deps)),
        out_specs=[ANY] * count,
        out_shape=[jax.ShapeDtypeStruct(a.shape, a.dtype) for a in arrays],
        input_output_aliases={i: i for i in range(count)},
        compiler_params=pltpu.CompilerParams(vmem_limit_bytes=1024 * 1024),
        cost_estimate=cost(0, 0, 0),
        name="after",
    )(*arrays, *deps)


def split_kernel(count, seq_ref, *refs):
    for i in range(count):
        refs[count + i][...] = refs[i][...]


def split_heads(my_seq, laid, count):
    tok, width = laid.shape
    cols = width // (3 * count)

    def source(hop):
        return pl.BlockSpec((tok, cols), lambda w, seq: (0, w * count + (seq[0] ^ hop)))

    return pl.pallas_call(
        functools.partial(split_kernel, count),
        grid_spec=pltpu.PrefetchScalarGridSpec(
            num_scalar_prefetch=1,
            grid=(3,),
            in_specs=[source(hop) for hop in range(count)],
            out_specs=[pl.BlockSpec((tok, cols), lambda w, seq: (0, w))] * count,
        ),
        out_shape=[jax.ShapeDtypeStruct((tok, 3 * cols), laid.dtype)] * count,
        compiler_params=params(),
        cost_estimate=cost(0, 4 * tok * width, 0),
        name="split_heads",
    )(my_seq.reshape(1), *([laid] * count))


def attend_kernel(count, *refs):
    parts, outs = refs[: 3 * count], refs[3 * count :]
    block = outs[0].shape[0]
    query, key, value = (
        jnp.concatenate([p[...] for p in parts[w * count : (w + 1) * count]], axis=0)
        for w in range(3)
    )
    scores = lax.dot_general(
        query, key, (((1,), (1,)), ((), ())), preferred_element_type=jnp.float32
    ) * HEAD_DIM ** (-0.5)
    top = jnp.max(scores, axis=-1, keepdims=True)
    grown = jnp.exp(scores - top)
    total = jnp.sum(grown, axis=-1, keepdims=True)
    mixed = jnp.dot(grown.astype(jnp.bfloat16), value, preferred_element_type=jnp.float32)
    mixed = (mixed / total).astype(jnp.bfloat16)
    for i in range(count):
        outs[i][...] = mixed[i * block : (i + 1) * block]


def attend(blocks, head_local):
    count = len(blocks)
    tok = blocks[0].shape[0]
    clip_len = count * tok

    def part(which):
        return pl.BlockSpec((tok, HEAD_DIM), lambda h: (0, which * head_local + h))

    return pl.pallas_call(
        functools.partial(attend_kernel, count),
        grid=(head_local,),
        in_specs=[part(which) for which in range(3) for _ in range(count)],
        out_specs=[pl.BlockSpec((tok, HEAD_DIM), lambda h: (0, h))] * count,
        out_shape=[jax.ShapeDtypeStruct((tok, head_local * HEAD_DIM), jnp.bfloat16)] * count,
        compiler_params=params(),
        cost_estimate=cost(
            4 * head_local * clip_len * clip_len * HEAD_DIM,
            8 * clip_len * head_local * HEAD_DIM,
            head_local * clip_len * clip_len,
        ),
        name="attend",
    )(*(list(blocks) * 3))


def project_kernel(count, seq_ref, *refs):
    parts = refs[:count]
    weight_ref, res_ref, gain_ref, mid_ref, norm_ref, acc_ref = refs[count:]
    step = pl.program_id(0)
    for i in range(count):

        @pl.when(step == i)
        def _(i=i):
            term = jnp.dot(parts[i][...], weight_ref[...], preferred_element_type=jnp.float32)
            acc_ref[...] = (res_ref[...].astype(jnp.float32) if i == 0 else acc_ref[...]) + term

    @pl.when(step == count - 1)
    def _():
        middle = acc_ref[...].astype(jnp.bfloat16)
        mid_ref[...] = middle
        mid_float = middle.astype(jnp.float32)
        mean = jnp.mean(mid_float * mid_float, axis=-1, keepdims=True)
        norm_ref[...] = (mid_float * lax.rsqrt(mean + 1e-06) * gain_ref[...]).astype(
            jnp.bfloat16
        )


def project(my_seq, parts, weight, residual, gain):
    count = len(parts)
    tok, depth = parts[0].shape
    width = weight.shape[1]
    out = jax.ShapeDtypeStruct((tok, width), jnp.bfloat16)
    return pl.pallas_call(
        functools.partial(project_kernel, count),
        grid_spec=pltpu.PrefetchScalarGridSpec(
            num_scalar_prefetch=1,
            grid=(count,),
            in_specs=[whole((tok, depth))] * count
            + [
                pl.BlockSpec((depth, width), lambda k, seq: (seq[0] ^ k, 0)),
                whole((tok, width)),
                whole((1, width)),
            ],
            out_specs=[whole((tok, width))] * 2,
            scratch_shapes=[pltpu.VMEM((tok, width), jnp.float32)],
        ),
        out_shape=[out, out],
        compiler_params=params(),
        cost_estimate=cost(2 * tok * count * depth * width, 2 * count * depth * width, 0),
        name="project",
    )(
        my_seq.reshape(1),
        *parts,
        pltpu.with_memory_space_constraint(weight, pltpu.HBM),
        residual,
        gain.reshape(1, width),
    )


def slot_kernel(hop, chips, place_ref, mine_ref, *rest):
    outs = rest[-chips:]
    piece = outs[0].shape[0]
    place = place_ref[hop]
    row = lax.broadcasted_iota(jnp.int32, (chips * piece, place.shape[-1]), 0)
    others = rest[:TRADES]
    halves = []
    for which in range(2):
        hit = (row == place[2 * which : 2 * which + 1]) | (
            row == place[2 * which + 1 : 2 * which + 2]
        )
        halves.append(jnp.where(hit, 1.0, 0.0).astype(jnp.bfloat16))
    slotted = jnp.dot(
        jnp.concatenate(halves, axis=1),
        jnp.concatenate([mine_ref[...]] + [o[...] for o in others], axis=0),
        preferred_element_type=jnp.float32,
    ).astype(jnp.bfloat16)
    for step in range(chips):
        outs[step][...] = slotted[step * piece : (step + 1) * piece]


def to_slots(hop, chips, piece, place, mine, others, deps):
    tok, width = mine.shape
    return pl.pallas_call(
        functools.partial(slot_kernel, hop, chips),
        in_specs=[whole(place.shape), whole(mine.shape)]
        + [whole(o.shape) for o in others]
        + [ANY] * len(deps),
        out_specs=[whole((piece, width))] * chips,
        out_shape=[jax.ShapeDtypeStruct((piece, width), jnp.bfloat16)] * chips,
        compiler_params=params(),
        cost_estimate=cost(4 * chips * piece * tok * width, 2 * width * (2 * tok + chips * piece), 0),
        name=f"slots{hop}",
    )(place, mine, *others, *deps)


def expert_kernel(chips, n_deps, *refs):
    pieces = refs[:chips]
    gate_hbm, up_hbm, down_hbm = refs[chips : chips + 3]
    outs = refs[chips + 3 + n_deps : 2 * chips + 3 + n_deps]
    rows_ref, hid_ref, gate_ref, up_ref, down_ref, sem = refs[-6:]
    piece = pieces[0].shape[0]
    hid, width = down_ref.shape
    hid_tiles = [slice(at, min(at + HID_TILE, hid)) for at in range(0, hid, HID_TILE)]
    out_tiles = [slice(at, at + OUT_TILE) for at in range(0, width, OUT_TILE)]
    stages = [[(gate_hbm, gate_ref, t), (up_hbm, up_ref, t)] for t in hid_tiles]
    stages += [[(down_hbm, down_ref, t)] for t in out_tiles]
    copies, count = [], 0
    for stage in stages:
        group = []
        for source, target, tile in stage:
            group.append(
                pltpu.make_async_copy(source.at[:, tile], target.at[:, tile], sem.at[count])
            )
            count += 1
        copies.append(group)

    def start(n):
        if n < len(copies):
            for copy in copies[n]:
                copy.start()

    def wait(n):
        for copy in copies[n]:
            copy.wait()
        start(n + AHEAD)

    for n in range(AHEAD):
        start(n)
    for i in range(chips):
        rows_ref[i * piece : (i + 1) * piece, :] = pieces[i][...]
    for n, tile in enumerate(hid_tiles):
        wait(n)
        gate_val = jnp.dot(rows_ref[...], gate_ref[:, tile], preferred_element_type=jnp.float32)
        up_val = jnp.dot(rows_ref[...], up_ref[:, tile], preferred_element_type=jnp.float32)
        hidden = gate_val / (1.0 + jnp.exp(-gate_val)) * up_val
        hid_ref[:, tile] = hidden.astype(jnp.bfloat16)
    for n, tile in enumerate(out_tiles):
        wait(len(hid_tiles) + n)
        out = jnp.dot(hid_ref[...], down_ref[:, tile], preferred_element_type=jnp.float32)
        out = out.astype(jnp.bfloat16)
        for i in range(chips):
            outs[i][:, tile] = out[i * piece : (i + 1) * piece]


def expert(hop, pieces, gate_mat, up_mat, down_mat, deps):
    chips = len(pieces)
    piece, width = pieces[0].shape
    hid = gate_mat.shape[-1]
    rows = chips * piece
    in_vmem = pl.BlockSpec(memory_space=pltpu.VMEM)
    in_hbm = pl.BlockSpec(memory_space=pltpu.HBM)
    n_sems = 2 * -(-hid // HID_TILE) + width // OUT_TILE
    return pl.pallas_call(
        functools.partial(expert_kernel, chips, len(deps)),
        in_specs=[in_vmem] * chips + [in_hbm] * 3 + [ANY] * len(deps),
        out_specs=[in_vmem] * chips,
        out_shape=[jax.ShapeDtypeStruct((piece, width), jnp.bfloat16)] * chips,
        scratch_shapes=[
            pltpu.VMEM((rows, width), jnp.bfloat16),
            pltpu.VMEM((rows, hid), jnp.bfloat16),
            pltpu.VMEM((width, hid), jnp.bfloat16),
            pltpu.VMEM((width, hid), jnp.bfloat16),
            pltpu.VMEM((hid, width), jnp.bfloat16),
            pltpu.SemaphoreType.DMA((n_sems,)),
        ],
        compiler_params=pltpu.CompilerParams(vmem_limit_bytes=32 * 1024 * 1024),
        cost_estimate=cost(6 * rows * width * hid, 6 * width * hid, rows * hid),
        name=f"expert{hop}",
    )(
        *pieces,
        *(pltpu.with_memory_space_constraint(w, pltpu.HBM) for w in (gate_mat, up_mat, down_mat)),
        *deps,
    )


def combine_kernel(hop, chips, n_deps, place_ref, gates_ref, *refs):
    pieces = refs[:chips]
    mine_ref, other_ref = refs[chips + n_deps :]
    rows = jnp.concatenate([p[...] for p in pieces], axis=0)
    place = place_ref[hop]
    gates = gates_ref[hop]
    column = lax.broadcasted_iota(jnp.int32, (place.shape[0], rows.shape[0]), 1)
    for which, out_ref in ((0, mine_ref), (1, other_ref)):
        total = 0.0
        for choice in range(TOP):
            at = 2 * which + choice
            picking = jnp.where(column == place[:, at : at + 1], 1.0, 0.0).astype(jnp.bfloat16)
            picked = jnp.dot(picking, rows, preferred_element_type=jnp.float32)
            total = total + picked * gates[:, at : at + 1]
        out_ref[...] = total.astype(out_ref.dtype)


def combine(hop, pieces, place, gates, deps):
    chips = len(pieces)
    piece, width = pieces[0].shape
    tok = place.shape[1]
    tile = pl.BlockSpec((tok, OUT_TILE), lambda i: (0, i))
    return pl.pallas_call(
        functools.partial(combine_kernel, hop, chips, len(deps)),
        grid=(width // OUT_TILE,),
        in_specs=[whole(place.shape), whole(gates.shape)]
        + [pl.BlockSpec((piece, OUT_TILE), lambda i: (0, i))] * chips
        + [ANY] * len(deps),
        out_specs=[tile, tile],
        out_shape=[
            jax.ShapeDtypeStruct((tok, width), jnp.float32),
            jax.ShapeDtypeStruct((tok, width), jnp.bfloat16),
        ],
        compiler_params=params(),
        cost_estimate=cost(COVER * 8 * tok * chips * piece * width, COVER * 2 * width * (chips * piece + 3 * tok), 0),
        name=f"combine{hop}",
    )(place, gates, *pieces, *deps)


def per_device(
    attn_inputs,
    residual,
    out_weight,
    norm_gain,
    expert_ids,
    gate_weights,
    gate_weight,
    up_weight,
    down_weight,
):
    tok_count = attn_inputs.shape[1]
    seq_count = lax.axis_size("seq")
    expert_count = lax.axis_size("exp")
    chips = expert_count // 2
    my_seq = lax.axis_index("seq")
    my_exp = lax.axis_index("exp")
    my_core, my_chip = my_exp % 2, my_exp // 2
    model_width = residual.shape[-1]
    head_local = HEADS // seq_count
    capacity = 5 * tok_count // (2 * expert_count)
    piece = -(-2 * capacity // 16) * 16

    def over_seq(value, hop):
        return lax.ppermute(value, "seq", xor_pairs(seq_count, hop))

    def over_chips(value, step):
        return lax.ppermute(value, "exp", xor_pairs(expert_count, 2 * step))

    def over_cores(value):
        return lax.ppermute(value, "exp", xor_pairs(expert_count, 1))

    gate_mat, up_mat, down_mat = gate_weight[0], up_weight[0], down_weight[0]

    def trade(value):
        part = value.shape[0] // TRADES
        return [over_cores(value[i * part : (i + 1) * part]) for i in range(TRADES)]

    blocks = split_heads(my_seq, attn_inputs.reshape(tok_count, 3 * HEADS * HEAD_DIM), seq_count)
    blocks = [over_seq(part, hop) if hop else part for hop, part in enumerate(blocks)]
    attended = attend(blocks, head_local)
    merged = [over_seq(p, hop) if hop else p for hop, p in enumerate(attended)]

    route_ids = expert_ids.reshape(tok_count * TOP)
    one_hot = (
        route_ids[:, None] == jnp.arange(expert_count, dtype=jnp.int32)[None, :]
    ).astype(jnp.int32)
    before = jnp.cumsum(one_hot, axis=0) - one_hot
    slot_ids = jnp.sum(before * one_hot, axis=-1)
    target = (route_ids * capacity + slot_ids).reshape(tok_count, TOP)
    route = jnp.concatenate([target.astype(jnp.float32), gate_weights[0]], axis=1).T
    (route_out,) = after([route], [blocks[1]])
    routes = [route] + [over_seq(route_out, hop) for hop in range(1, seq_count)]
    in_middle = (my_seq == 1) | (my_seq == 2)
    route = jnp.stack(
        [
            routes[0],
            routes[1],
            jnp.where(in_middle, routes[3], routes[2]),
            jnp.where(in_middle, routes[2], routes[3]),
        ]
    )
    both = jnp.concatenate([route, over_cores(route)], axis=1)
    goal = jnp.concatenate([both[:, :TOP], both[:, 2 * TOP : 3 * TOP]], axis=1).astype(jnp.int32)
    gates = jnp.concatenate([both[:, TOP : 2 * TOP], both[:, 3 * TOP :]], axis=1)
    goal_exp = goal // capacity
    clip = (jnp.arange(2 * TOP, dtype=jnp.int32) // TOP)[None, :, None]
    place = jnp.where(
        goal_exp % 2 == my_core,
        ((goal_exp // 2) ^ my_chip) * piece + clip * capacity + goal % capacity,
        -1,
    )
    place_t = place.transpose(0, 2, 1)
    gates_t = gates.transpose(0, 2, 1)

    all_weight = lax.all_gather(out_weight, "exp", axis=0, tiled=True)
    middle, normed = project(
        my_seq, merged, all_weight, residual.reshape(tok_count, model_width), norm_gain
    )
    mid_float = middle.astype(jnp.float32)

    def dispatch(hop, block, deps):
        pieces = to_slots(hop, chips, piece, place, block, trade(block), deps)
        return [over_chips(p, s) if s else p for s, p in enumerate(pieces)], pieces[0]

    def run(hop, deps):
        return expert(hop, arrived[hop], gate_mat, up_mat, down_mat, deps)

    def give_back(hop, partial, after_deps, deps):
        if after_deps:
            partial = after(partial, after_deps)
        returned = [over_chips(p, s) if s else p for s, p in enumerate(partial)]
        mine, other = combine(hop, returned, place_t, gates_t, deps)
        total = mine + over_cores(other).astype(jnp.float32)
        return total, total.astype(jnp.bfloat16)

    def joined(total, received):
        return (total + received.astype(jnp.float32)).astype(jnp.bfloat16)

    def hop_along(value, pairs):
        return lax.ppermute(value, "seq", pairs)

    arrived = {}
    arrived[0], own0 = dispatch(0, normed, [])
    (normed_out,) = after([normed], [own0])
    pair_block = hop_along(normed_out, PAIRS)
    cross_block = hop_along(normed_out, CROSS)
    cross_pair = hop_along(pair_block, CROSS)
    arrived[1], own1 = dispatch(1, pair_block, arrived[0][1:2])
    done0 = run(0, [own1])
    (kept,) = after([cross_block], [done0[0]])
    second = jnp.where(in_middle, kept, hop_along(cross_block, OUT))
    arrived[2], own2 = dispatch(2, second, [done0[0]] + arrived[1][1:2])
    done1 = run(1, [own2])
    (kept,) = after([cross_pair], [done1[0]])
    third = jnp.where(in_middle, kept, hop_along(cross_pair, OUT))
    arrived[3], own3 = dispatch(3, third, [done1[0]])
    done2 = run(2, [own3])
    done3 = run(3, [done2[0]])
    total2, send2 = give_back(2, done2, [], [done3[0]])
    in2 = hop_along(send2, IN)
    next2 = joined(total2, in2)
    back2 = hop_along(next2, CROSS)
    total3, send3 = give_back(3, done3, [], [send2])
    in3 = hop_along(send3, IN)
    next3 = joined(total3, in3)
    back3 = hop_along(next3, FAR)
    total1, send1 = give_back(1, done1, [], [send3, next2])
    back1 = hop_along(send1, PAIRS)
    result, _ = give_back(0, done0, [], [send1])
    result = mid_float + result
    for back in (back1, back2, back3):
        result = result + back.astype(jnp.float32)
    return result.astype(jnp.bfloat16).reshape(1, tok_count, model_width)


def solution(mesh):
    placed = (
        P("exp", "seq", None),
        P("exp", "seq", None),
        P("exp", None),
        P(),
        P("exp", "seq", None),
        P("exp", "seq", None),
        P("exp", None, "seq"),
        P("exp", None, "seq"),
        P("exp", "seq", None),
    )
    return jax.shard_map(
        per_device, mesh=mesh, in_specs=placed, out_specs=P("exp", "seq", None), check_vma=False
    )
```
